32 devices in a mesh: groups: 2 (over x), node: 16 (over z, y, core), local: 1.
Axes of the slice: x: 2, y: 2, z: 4, core: 2. Of those that a mesh axis runs over, the one named last changes fastest.
Arguments:
- resid: bfloat16 [256, 3584], P(('groups', 'node', 'local')), parts along dimension 0, may hold values from -16 to 16
- prev_rows: bfloat16 [32, 1, 16, 4, 3584], P(('groups', 'node'), 'local'), parts along dimension 0, may hold values from -6 to 6
- prev_slots: int32 [256, 4], P(('groups', 'node', 'local')), parts along dimension 0, may hold values from 0 to 15, all different within a row; in each aligned block of 8 rows (0 to 7, 8 to 15, ...) at most 4 rows name the same one
- prev_gates: float32 [256, 4], P(('groups', 'node', 'local')), parts along dimension 0, may hold values from 0.1 to 0.9
- query: bfloat16 [256, 64, 576], P(('groups', 'node', 'local')), parts along dimension 0, may hold values from -8 to 8
- cache: bfloat16 [256, 192, 576], P(('groups', 'node', 'local')), parts along dimension 0, may hold values from -4 to 4
- lengths: int32 [256], P(('groups', 'node', 'local')), parts along dimension 0, may hold values from 24 to 192, as said below
- norm_gain: float32 [3584], replicated, may hold values from 0.1 to 1.9
- router: bfloat16 [3584, 14], replicated, may hold values from -0.09375 to 0.09375
- slot_expert: int32 [16], replicated, may hold values from 0 to 13, as said below
- expert_ids: int32 [256, 4], P(('groups', 'node', 'local')), parts along dimension 0, may hold values from 0 to 13, all different within a row; in each aligned block of 8 rows (0 to 7, 8 to 15, ...) at most 4 rows name the same one
- gate_up: bfloat16 [16, 3584, 2, 1024], P('node', None, None, 'local')
- down: bfloat16 [16, 1024, 3584], P('node', 'local')
Outputs:
- attended: bfloat16 [256, 64, 512], P(('groups', 'node', 'local')), parts along dimension 0
- mixed_out: bfloat16 [256, 3584], P(('groups', 'node', 'local')), parts along dimension 0
The draws below stay inside these ranges and needn't reach their ends.
There are 2 independent parts, one for each index of `groups`. The reference program is written for one: setup_inputs(seed, part) draws one part's arguments, and reference() takes and returns one part's arrays. A program takes and returns all parts, laid end to end along the dimension named above; an argument that names none is the same for every part. Nothing has to cross between parts.
Inputs may be any that keep to these rules, and one draw needn't show every extreme that they name: `slot_expert`: each of the 14 experts sits in one slot or two; 2 of them sit in two. `prev_slots`: each row names 4 different slots; at most 4 rows of one device name one slot, and that many do in some device. `expert_ids`: each row names 4 different experts; at most 4 rows of one device name one expert, and that many do in some device. `lengths`: every device holds a request whose length is 192.
All inputs are finite; a program needn't handle non-finite values.
Results may differ from the reference program's by a relative error of at most 0.005.
Values may be sent and summed in bfloat16 or wider, within the bound.
A program may use at most 128 MiB of HBM per device.

```python
import math
import jax
import jax.numpy as jnp
import numpy as np
from jax import lax

D = 3584
FF = 1024
HEADS = 64
LATENT = 512
ROPE = 64
NOPE = 128
TOP = 4
R = 8
LEN = 192
SLOTS = 16
EXPERTS = 14
CAP = 4
TOKENS = 128
N_LOCAL = 1


def slot_table(key):
    key = jax.random.fold_in(key, 11)
    first_key, second_key = jax.random.split(key)
    shuffled = jax.random.permutation(first_key, SLOTS)
    folded = jnp.where(shuffled < EXPERTS, shuffled, shuffled - EXPERTS)
    relabel = jax.random.permutation(second_key, EXPERTS)
    return relabel[folded].astype(jnp.int32)


def draw_slot_expert(key, part):
    return slot_table(key)


def draw_gate_up(key, part):
    placement = slot_table(key)
    key = jax.random.fold_in(key, 2)

    def expert_block(expert):
        sample_values = jax.random.normal(jax.random.fold_in(key, expert), (D, 2, FF), jnp.float32)
        return (sample_values * D ** (-0.5)).astype(jnp.bfloat16)
    return lax.map(expert_block, placement)


def draw_down(key, part):
    placement = slot_table(key)
    key = jax.random.fold_in(key, 3)

    def expert_block(expert):
        sample_values = jax.random.normal(jax.random.fold_in(key, expert), (FF, D), jnp.float32)
        return (sample_values * FF ** (-0.5)).astype(jnp.bfloat16)
    return lax.map(expert_block, placement)


def draw_lengths(key, part):
    key = jax.random.fold_in(key, 5)
    base_key, pick_key = jax.random.split(key)
    base_lengths = jax.random.randint(base_key, (TOKENS,), LEN // 8, LEN + 1)
    picked = jax.random.randint(pick_key, (TOKENS // R,), 0, R)
    full_row = jnp.arange(TOKENS) % R == jnp.repeat(picked, R)
    return jnp.where(full_row, LEN, base_lengths).astype(jnp.int32)


def draw_cache(key, part):
    key = jax.random.fold_in(key, 6)
    sample_values = jax.random.normal(key, (TOKENS, LEN, LATENT + ROPE), jnp.float32)
    return jnp.clip(sample_values, -4.0, 4.0).astype(jnp.bfloat16)


def draw_query(key, part):
    key = jax.random.fold_in(key, 7)
    sample_values = jax.random.normal(key, (TOKENS, HEADS, LATENT + ROPE), jnp.float32)
    return jnp.clip(sample_values, -4.0, 4.0).astype(jnp.bfloat16)


def draw_resid(key, part):
    key = jax.random.fold_in(key, 8)
    sample_values = jax.random.normal(key, (TOKENS, D), jnp.float32)
    return jnp.clip(sample_values, -5.0, 5.0).astype(jnp.bfloat16)


def block_scale(stream_key, dims, shards, low, high):
    gain = 1.0
    for position, parts in shards:
        steps = jax.random.uniform(jax.random.fold_in(jax.random.fold_in(stream_key, 6), position), (parts,), jnp.float32, low / len(shards), high / len(shards))
        gain = gain * jnp.repeat(jnp.exp(steps), dims[position] // parts).reshape((-1,) + (1,) * (len(dims) - 1 - position))
    return gain


def deal_out(rng, own, number, rows, count, top, most, slope):
    order = jax.random.permutation(rng, count)
    crowded, ordinary = shares(count, rows * top, most, slope, True), shares(count, rows * top, most, slope, False)
    places = jnp.arange(count)

    def named(sizes, rotation):
        used = int((sizes > 0).sum())
        fixed = max(1, used // 4)
        shifted = fixed + (places - fixed + rotation * (used - fixed)) % max(1, count - fixed)
        return jnp.zeros((count,), jnp.int32).at[order[jnp.where(places < fixed, places, shifted)]].set(jnp.asarray(sizes, jnp.int32))

    sizes = jnp.where(number % 4 == 0, named(crowded, number // 4), named(ordinary, number - number // 4 - 1))
    mixed = jax.random.permutation(jax.random.fold_in(own, 3), count)
    source_of, receiver = mixed[0:count // 2 * 2:2], mixed[1:count // 2 * 2:2]
    slack = jnp.minimum(sizes[source_of] - 1, most - sizes[receiver]) // 2
    slack = jnp.where((source_of == order[0]) | (receiver == order[0]) | (sizes[receiver] == 0), 0, jnp.maximum(slack, 0))
    shifted = jax.random.randint(jax.random.fold_in(own, 4), (count // 2,), 0, 1 << 20) % (slack + 1)
    sizes = sizes.at[source_of].add(-shifted).at[receiver].add(shifted)
    members = jnp.searchsorted(jnp.cumsum(sizes), jnp.arange(rows * top), side="right").astype(jnp.int32)
    listing = members.reshape(top, rows).T
    listing = listing[jax.random.permutation(jax.random.fold_in(own, 1), rows)]
    rotation = jax.random.randint(jax.random.fold_in(own, 2), (rows, 1), 0, top)
    return jnp.take_along_axis(listing, (jnp.arange(top)[None, :] + rotation) % top, axis=1)


def shares(amount, total, reach, skew, full):
    portions = [(1 << 20) // math.isqrt(standing ** skew) + 1 for standing in range(1, amount + 1)]
    largest = reach if full else min(reach, max(-(-total // amount), total * portions[0] // sum(portions)))
    least = 1 if total - largest >= amount - 1 else 0
    given, surplus = [largest] + [least] * (amount - 1), total - largest - least * (amount - 1)
    while surplus > 0:
        candidates = [i for i in range(1, amount) if given[i] < largest] or [i for i in range(1, amount) if given[i] < reach]
        mass, remaining = sum([portions[i] for i in candidates]), surplus
        for i in candidates:
            more = min(reach - given[i], max(1, remaining * portions[i] // mass), surplus)
            given[i] = given[i] + more
            surplus = surplus - more
    return np.array(given)


def centred(rng, dims, scale, limit, shards=(), kind=jnp.bfloat16):
    entries = jax.random.normal(rng, dims, jnp.float32) * scale
    if len(shards) > 0:
        entries = block_scale(rng, dims, shards, -0.22, 0.18) * entries
    return jnp.clip(entries, min=-limit, max=limit).astype(kind)


def setup_inputs(seed: int = 0, part: int = 0) -> dict:
    arg_keys = jax.random.split(jax.random.key(seed), 14)
    part_splits = jax.random.split(jax.random.fold_in(arg_keys[13], part), 14)
    resid = draw_resid(jax.random.fold_in(jax.random.fold_in(arg_keys[13], part), 71), part)
    prev_rows = centred(part_splits[1], (SLOTS, N_LOCAL, SLOTS, CAP, D), 1.0, 6.0, ((0, 16),))
    prev_slots_keys = jax.random.split(jax.random.fold_in(part_splits[2], 1), TOKENS // R)
    prev_slots_turns = jax.random.permutation(jax.random.fold_in(part_splits[2], 3), TOKENS // R)
    prev_slots = jax.vmap(lambda own, number: deal_out(jax.random.fold_in(part_splits[2], 2), own, number, R, SLOTS, TOP, CAP, 1))(prev_slots_keys, prev_slots_turns).reshape((TOKENS, TOP))
    prev_gates = jnp.clip(0.1 + 0.79999997 * jax.random.uniform(part_splits[3], (TOKENS, TOP), jnp.float32) ** block_scale(part_splits[3], (TOKENS, TOP), ((0, 16),), -0.2, 0.2), 0.1, 0.9)
    query = draw_query(jax.random.fold_in(jax.random.fold_in(arg_keys[13], part), 71), part)
    cache = draw_cache(jax.random.fold_in(jax.random.fold_in(arg_keys[13], part), 71), part)
    lengths = draw_lengths(jax.random.fold_in(jax.random.fold_in(arg_keys[13], part), 71), part)
    norm_gain = jnp.clip(1.0 + 0.18 * jax.random.normal(arg_keys[7], (D,), jnp.float32), 0.1, 1.9)
    router = centred(arg_keys[8], (D, EXPERTS), D ** -0.5, 0.09375)
    slot_expert = draw_slot_expert(jax.random.fold_in(arg_keys[13], 71), part)
    expert_ids_keys = jax.random.split(jax.random.fold_in(part_splits[10], 1), TOKENS // R)
    expert_ids_turns = jax.random.permutation(jax.random.fold_in(part_splits[10], 3), TOKENS // R)
    expert_ids = jax.vmap(lambda own, number: deal_out(jax.random.fold_in(part_splits[10], 2), own, number, R, EXPERTS, TOP, CAP, 2))(expert_ids_keys, expert_ids_turns).reshape((TOKENS, TOP))
    gate_up = draw_gate_up(jax.random.fold_in(arg_keys[13], 71), part)
    down = draw_down(jax.random.fold_in(arg_keys[13], 71), part)
    return {"resid": resid, "prev_rows": prev_rows, "prev_slots": prev_slots, "prev_gates": prev_gates, "query": query, "cache": cache, "lengths": lengths, "norm_gain": norm_gain, "router": router, "slot_expert": slot_expert, "expert_ids": expert_ids, "gate_up": gate_up, "down": down}


def slot_places(targets):
    pair_count = targets.shape[1]
    same_slot = (targets[:, :, None] == targets[:, None, :]).astype(jnp.int32)
    earlier = (jnp.arange(pair_count)[None, :] < jnp.arange(pair_count)[:, None]).astype(jnp.int32)
    return lax.optimization_barrier(jnp.sum(same_slot * earlier[None], axis=2)).astype(jnp.int32)

def reference(resid, prev_rows, prev_slots, prev_gates, query, cache, lengths, norm_gain, router, slot_expert, expert_ids, gate_up, down):
    device_count = SLOTS * N_LOCAL
    pair_count = R * TOP
    targets = prev_slots.reshape(device_count, pair_count).astype(jnp.int32)
    places = slot_places(targets)
    owner = jnp.arange(device_count, dtype=jnp.int32)[:, None] + jnp.zeros((1, pair_count), jnp.int32)
    owner_node = (owner // N_LOCAL).astype(jnp.int32)
    owner_local = (owner % N_LOCAL).astype(jnp.int32)
    values = prev_rows[targets, owner_local, owner_node, places]
    values = values.astype(jnp.float32).reshape(TOKENS, TOP, D)
    residual = resid.astype(jnp.float32) + lax.optimization_barrier(jnp.sum(prev_gates[:, :, None] * values, axis=1))
    mean_square = lax.optimization_barrier(jnp.mean(residual * residual, axis=1, keepdims=True))
    normed = (residual * lax.rsqrt(mean_square + 1e-06) * norm_gain[None, :]).astype(jnp.bfloat16)
    logits = jnp.dot(normed, router, preferred_element_type=jnp.float32)
    picked = jnp.take_along_axis(logits, expert_ids, axis=1)
    score = jax.nn.sigmoid(picked)
    gate_weight = 2.5 * score / lax.optimization_barrier(jnp.sum(score, axis=1, keepdims=True))

    def per_expert(total, expert):
        slot = jnp.argmax(slot_expert == expert).astype(jnp.int32)
        weights_in = lax.dynamic_index_in_dim(gate_up, slot, 0, keepdims=False).reshape(D, 2 * FF)
        weights_out = lax.dynamic_index_in_dim(down, slot, 0, keepdims=False)
        projected = jnp.dot(normed, weights_in, preferred_element_type=jnp.float32)
        hidden = (jax.nn.silu(projected[:, :FF]) * projected[:, FF:]).astype(jnp.bfloat16)
        expert_out = jnp.dot(hidden, weights_out, preferred_element_type=jnp.float32).astype(jnp.bfloat16)
        expert_out = lax.optimization_barrier(expert_out).astype(jnp.float32)
        share = lax.optimization_barrier(jnp.sum(jnp.where(expert_ids == expert, gate_weight, 0.0), axis=1))
        return (total + share[:, None] * expert_out, None)
    routed, _ = lax.scan(per_expert, jnp.zeros((TOKENS, D), jnp.float32), jnp.arange(EXPERTS, dtype=jnp.int32))
    mixed_out = (residual + routed).astype(jnp.bfloat16)
    score_scale = (NOPE + ROPE) ** (-0.5)
    scores = jnp.einsum('thc,tlc->thl', query.astype(jnp.float32), cache.astype(jnp.float32)) * score_scale
    in_range = jnp.arange(LEN)[None, None, :] < lengths[:, None, None]
    scores = jnp.where(in_range, scores, -1e+30)
    row_max = lax.optimization_barrier(jnp.max(scores, axis=2, keepdims=True))
    expo = jnp.where(in_range, jnp.exp(scores - row_max), 0.0)
    weights = (expo / lax.optimization_barrier(jnp.sum(expo, axis=2, keepdims=True))).astype(jnp.bfloat16)
    attended = jnp.einsum('thl,tlc->thc', weights.astype(jnp.float32), cache[:, :, :LATENT].astype(jnp.float32))
    return (attended.astype(jnp.bfloat16), mixed_out)
```

```python
import functools

import jax
import jax.numpy as jnp
from jax import lax
from jax.experimental import pallas as pl
from jax.experimental.pallas import tpu as pltpu
from jax.sharding import PartitionSpec as P

LATENT = 512
ROPE = 64
NOPE = 128


def slot_places(targets):
    pair_count = targets.shape[0]
    same_slot = (targets[:, None] == targets[None, :]).astype(jnp.int32)
    earlier = (jnp.arange(pair_count)[None, :] < jnp.arange(pair_count)[:, None]).astype(jnp.int32)
    return jnp.sum(same_slot * earlier, axis=1)


def selector(targets, places, slot_count, capacity):
    column = jnp.arange(slot_count * capacity, dtype=jnp.int32)[None, :]
    return (column == (targets * capacity + places)[:, None]).astype(jnp.bfloat16)


def expert_partial(gathered, gate_up, down):
    features = gathered.shape[-1]
    unit_count = down.shape[1]
    flat_rows = gathered.reshape(-1, features)
    projected = jnp.dot(
        flat_rows, gate_up.reshape(features, 2 * unit_count), preferred_element_type=jnp.float32
    )
    hidden = (jax.nn.silu(projected[:, :unit_count]) * projected[:, unit_count:]).astype(
        jnp.bfloat16
    )
    partial_value = jnp.dot(
        hidden, down.reshape(unit_count, features), preferred_element_type=jnp.float32
    )
    return partial_value.reshape(gathered.shape)


def shards(
    resid,
    prev_rows,
    prev_slots,
    prev_gates,
    query,
    cache,
    lengths,
    norm_gain,
    router,
    slot_expert,
    expert_ids,
    gate_up,
    down,
):
    slot_count = lax.axis_size("node")
    core_count = lax.axis_size("local")
    row_count, features = resid.shape
    top_k = expert_ids.shape[1]
    pair_count = row_count * top_k
    capacity = prev_rows.shape[3]
    returned = lax.all_to_all(
        prev_rows.reshape(slot_count, capacity, features),
        "node",
        split_axis=0,
        concat_axis=0,
        tiled=True,
    )
    prev_targets = prev_slots.reshape(pair_count)
    prev_pick = selector(prev_targets, slot_places(prev_targets), slot_count, capacity)
    values = jnp.dot(
        prev_pick,
        returned.reshape(slot_count * capacity, features),
        preferred_element_type=jnp.float32,
    )
    values = values.reshape(row_count, top_k, features)
    residual = resid.astype(jnp.float32) + jnp.sum(prev_gates[:, :, None] * values, axis=1)
    mean_square = jnp.mean(residual * residual, axis=1, keepdims=True)
    normed = (residual * lax.rsqrt(mean_square + 1e-06) * norm_gain[None, :]).astype(jnp.bfloat16)
    logits = jnp.dot(normed, router, preferred_element_type=jnp.float32)
    expert_count = router.shape[1]
    chosen = expert_ids[:, :, None] == jnp.arange(expert_count, dtype=jnp.int32)[None, None, :]
    picked = jnp.sum(jnp.where(chosen, logits[:, None, :], 0.0), axis=2)
    score = jax.nn.sigmoid(picked)
    gate_weight = 2.5 * score / jnp.sum(score, axis=1, keepdims=True)
    flat_ids = expert_ids.reshape(pair_count)
    holds_it = slot_expert[None, :] == flat_ids[:, None]
    slot_index = jnp.arange(slot_count, dtype=jnp.int32)[None, :]
    targets = jnp.min(jnp.where(holds_it, slot_index, slot_count), axis=1)
    pick = selector(targets, slot_places(targets), slot_count, capacity)
    repeated = jnp.broadcast_to(normed[:, None, :], (row_count, top_k, features)).reshape(
        pair_count, features
    )
    outgoing = jnp.einsum("pk,pd->kd", pick, repeated, preferred_element_type=jnp.float32).astype(
        jnp.bfloat16
    )
    outgoing = outgoing.reshape(slot_count, capacity, features)
    doubled = jnp.broadcast_to(outgoing[:, None], (slot_count, core_count, capacity, features))
    doubled = doubled.reshape(slot_count * core_count, capacity, features)
    arrived = lax.all_to_all(doubled, ("node", "local"), split_axis=0, concat_axis=0, tiled=True)
    gathered = arrived.reshape(slot_count, core_count, capacity, features)
    partial_value = expert_partial(gathered, gate_up, down)
    summed = lax.psum_scatter(partial_value, "local", scatter_dimension=1, tiled=True)
    expert_out = summed.astype(jnp.bfloat16).reshape(slot_count, capacity, features)
    came_back = lax.all_to_all(expert_out, "node", split_axis=0, concat_axis=0, tiled=True)
    outputs = jnp.dot(
        pick, came_back.reshape(slot_count * capacity, features), preferred_element_type=jnp.float32
    )
    outputs = outputs.reshape(row_count, top_k, features)
    routed = jnp.sum(gate_weight[:, :, None] * outputs, axis=1)
    mixed_out = (residual + routed).astype(jnp.bfloat16)
    score_scale = (NOPE + ROPE) ** (-0.5)
    scores = (
        jnp.einsum("thc,tlc->thl", query, cache, preferred_element_type=jnp.float32) * score_scale
    )
    positions = cache.shape[1]
    in_range = jnp.arange(positions)[None, None, :] < lengths[:, None, None]
    scores = jnp.where(in_range, scores, -1e30)
    row_max = jnp.max(scores, axis=2, keepdims=True)
    expo = jnp.where(in_range, jnp.exp(scores - row_max), 0.0)
    weights = (expo / jnp.sum(expo, axis=2, keepdims=True)).astype(jnp.bfloat16)
    attended = jnp.einsum(
        "thl,tlc->thc", weights, cache[:, :, :LATENT], preferred_element_type=jnp.float32
    )
    return (attended.astype(jnp.bfloat16), mixed_out)


LANES = 128
MESH = pl.DeviceIdType.MESH
F32 = jnp.float32
BF16 = jnp.bfloat16


def remote(src, dst, send_sem, recv_sem, peer):
    return pltpu.make_async_remote_copy(
        src_ref=src,
        dst_ref=dst,
        send_sem=send_sem,
        recv_sem=recv_sem,
        device_id={"node": peer},
        device_id_type=MESH,
    )


def columns_of(ref):
    top_k, rows = ref.shape
    values = ref[...].astype(F32)
    diagonal = lax.broadcasted_iota(jnp.int32, (rows, rows), 0) == lax.broadcasted_iota(
        jnp.int32, (rows, rows), 1
    )
    return [
        jnp.sum(
            jnp.where(diagonal, jnp.broadcast_to(values[k : k + 1, :], (rows, rows)), 0.0),
            axis=1,
            keepdims=True,
        )
        for k in range(top_k)
    ]


def fused_kernel(
    n,
    lengths_ref,
    slot_expert_ref,
    resid_ref,
    slots_ref,
    gates_ref,
    gain_ref,
    router_ref,
    ids_ref,
    prev_hbm,
    query_hbm,
    cache_hbm,
    gate_up_hbm,
    down_hbm,
    attended_hbm,
    mixed_ref,
    prev_in,
    prev_f32,
    query_v,
    cache_v,
    attended_v,
    wide_v,
    down_v,
    blocks,
    spread,
    hidden_v,
    partial_v,
    out_blocks,
    core_in,
    side_out,
    side_in,
    far_out,
    far_in,
    residual_v,
    local_sem,
    wide_sem,
    prev_send,
    prev_recv,
    gather_send,
    gather_recv,
    sum_send,
    sum_recv,
):
    me = lax.axis_index("node")
    depth = n // 4
    z, y, c = me // 4, (me // 2) % 2, me % 2
    rows, features = resid_ref.shape
    capacity = prev_hbm.shape[3]
    units = down_v.shape[0]
    strips = units // LANES

    query_copy = pltpu.make_async_copy(query_hbm, query_v, local_sem.at[0])
    cache_copy = pltpu.make_async_copy(cache_hbm, cache_v, local_sem.at[1])
    down_copy = pltpu.make_async_copy(down_hbm.at[0], down_v, local_sem.at[2])
    own_prev = pltpu.make_async_copy(prev_hbm.at[0, 0, me], prev_in.at[me], local_sem.at[3])

    def strip_copy(i):
        return pltpu.make_async_copy(
            gate_up_hbm.at[0, :, :, pl.ds(i * LANES, LANES)], wide_v.at[i], wide_sem.at[i]
        )

    query_copy.start()
    cache_copy.start()
    own_prev.start()

    barrier = pltpu.get_barrier_semaphore()

    def greet(step, carry):
        pl.semaphore_signal(
            barrier, inc=1, device_id={"node": lax.rem(me + step, n)}, device_id_type=MESH
        )
        return carry

    lax.fori_loop(1, n, greet, 0)
    pl.semaphore_wait(barrier, n - 1)

    def prev_copy(step):
        peer = lax.rem(me + step, n)
        return remote(
            prev_hbm.at[0, 0, peer], prev_in.at[me], prev_send.at[step], prev_recv.at[me], peer
        )

    def send_prev(step, carry):
        prev_copy(step).start()
        return carry

    lax.fori_loop(1, n, send_prev, 0)
    for i in range(strips):
        strip_copy(i).start()
    down_copy.start()

    query_copy.wait()
    cache_copy.wait()
    positions = cache_v.shape[1]
    heads = query_v.shape[1]

    def attend(r, carry):
        keys = cache_v[r]
        scores = lax.dot_general(
            query_v[r], keys, (((1,), (1,)), ((), ())), preferred_element_type=F32
        ) * ((NOPE + ROPE) ** (-0.5))
        live = lax.broadcasted_iota(jnp.int32, (heads, positions), 1) < lengths_ref[r]
        scores = jnp.where(live, scores, -1e30)
        row_max = jnp.max(scores, axis=1, keepdims=True)
        expo = jnp.where(live, jnp.exp(scores - row_max), 0.0)
        weights = (expo / jnp.sum(expo, axis=1, keepdims=True)).astype(BF16)
        attended_v[r] = jnp.dot(
            weights, keys[:, :LATENT], preferred_element_type=F32
        ).astype(BF16)
        return carry

    lax.fori_loop(0, query_v.shape[0], attend, 0)
    attended_copy = pltpu.make_async_copy(attended_v, attended_hbm, local_sem.at[4])
    attended_copy.start()

    width = n * capacity
    lane = lax.broadcasted_iota(jnp.int32, (rows, width), 1)
    lane_slot = (lane // capacity).astype(F32)
    lane_place = (lane % capacity).astype(F32)
    uses = jnp.zeros((rows, width), F32)
    gate_row = jnp.zeros((rows, width), F32)
    for slot, gate in zip(columns_of(slots_ref), columns_of(gates_ref)):
        hit = lane_slot == slot
        uses = uses + jnp.where(hit, 1.0, 0.0)
        gate_row = gate_row + jnp.where(hit, gate, 0.0)
    token = lax.broadcasted_iota(jnp.int32, (rows, width), 0)
    places = jnp.zeros((rows, width), F32)
    for t in range(rows - 1):
        places = places + jnp.where(token > t, uses[t : t + 1, :], 0.0)
    gate_row = jnp.where(places == lane_place, gate_row, 0.0)
    gate_high = gate_row.astype(BF16)
    rest = gate_row - gate_high.astype(F32)
    gate_mid = rest.astype(BF16)
    gate_low = (rest - gate_mid.astype(F32)).astype(BF16)

    slot_lane = lax.broadcasted_iota(jnp.int32, (1, LANES), 1)
    held = jnp.full((1, LANES), -1, jnp.int32)
    for i in range(n):
        held = jnp.where(slot_lane == i, slot_expert_ref[i], held)
    first = jnp.ones((1, LANES), F32)
    for i in range(n):
        first = jnp.where((held == slot_expert_ref[i]) & (slot_lane > i), 0.0, first)
    held = held.astype(F32)

    own_prev.wait()

    def take_prev(step, carry):
        source = lax.rem(me + step, n)
        remote(
            prev_hbm.at[0, 0, me], prev_in.at[source], prev_send.at[step], prev_recv.at[source],
            source,
        ).wait_recv()
        return carry

    lax.fori_loop(1, n, take_prev, 0)
    for i in range(n):
        prev_f32[i * capacity : (i + 1) * capacity, :] = prev_in[i].astype(F32)
    prev_rows = prev_f32[...].astype(BF16)
    combined = (
        jnp.dot(gate_high, prev_rows, preferred_element_type=F32)
        + jnp.dot(gate_mid, prev_rows, preferred_element_type=F32)
        + jnp.dot(gate_low, prev_rows, preferred_element_type=F32)
    )
    residual = resid_ref[...].astype(F32) + combined
    residual_v[...] = residual
    mean_square = jnp.sum(residual * residual, axis=1, keepdims=True) * (1.0 / features)
    normed = (residual * lax.rsqrt(mean_square + 1e-06) * gain_ref[...]).astype(BF16)
    logits = lax.dot_general(
        normed, router_ref[...], (((1,), (1,)), ((), ())), preferred_element_type=F32
    )
    expert_lane = lax.broadcasted_iota(jnp.int32, logits.shape, 1).astype(F32)
    ids = columns_of(ids_ref)
    picked = [
        jnp.sum(jnp.where(expert_lane == chosen, logits, 0.0), axis=1, keepdims=True)
        for chosen in ids
    ]
    score = [1.0 / (1.0 + jnp.exp(-value)) for value in picked]
    total = functools.reduce(lambda a, b: a + b, score)
    slot_weight = jnp.zeros((rows, LANES), F32)
    for chosen, value in zip(ids, score):
        slot_weight = slot_weight + jnp.where(held == chosen, 2.5 * value / total, 0.0)
    slot_weight = slot_weight * first
    weight_high = slot_weight.astype(BF16)
    weight_low = (slot_weight - weight_high.astype(F32)).astype(BF16)
    blocks[me, :, :features] = normed
    blocks[me, :, features : features + LANES] = weight_high
    blocks[me, :, features + LANES :] = weight_low

    across, sibling = z * 4 + (1 - y) * 2 + c, z * 4 + y * 2 + (1 - c)
    started = []

    def send_block(index, peer):
        copy = remote(
            blocks.at[index], blocks.at[index], gather_send.at[len(started)],
            gather_recv.at[index], peer,
        )
        copy.start()
        started.append(copy)

    def await_block(index):
        remote(
            blocks.at[index], blocks.at[index], gather_send.at[0], gather_recv.at[index], sibling
        ).wait_recv()

    for d in range(1, depth):
        send_block(me, lax.rem(z + d, depth) * 4 + y * 2 + c)
    send_block(me, across)
    send_block(me, sibling)
    await_block(across)
    send_block(across, sibling)
    for d in range(1, depth):
        other = lax.rem(z + d, depth) * 4 + y * 2 + c
        await_block(other)
        send_block(other, across)
        send_block(other, sibling)
    for d in range(1, depth):
        other = lax.rem(z + d, depth) * 4 + (1 - y) * 2 + c
        await_block(other)
        send_block(other, sibling)
    for d in range(depth):
        for side in range(2):
            await_block(lax.rem(z + d, depth) * 4 + side * 2 + (1 - c))
    for i in range(strips):
        strip_copy(i).wait()

    tokens = n * rows
    low = lax.broadcasted_iota(jnp.int32, (LANES, 4 * LANES), 0)
    high = lax.broadcasted_iota(jnp.int32, (LANES, 4 * LANES), 1)
    dealt = jnp.where(
        (high == 2 * low) | (high == 2 * low + 1 + 2 * LANES), 1.0, 0.0
    ).astype(BF16)
    for b in range(features // LANES):
        part = blocks[:, :, b * LANES : (b + 1) * LANES].astype(F32).reshape(tokens, LANES)
        both = jnp.dot(part.astype(BF16), dealt, preferred_element_type=F32).astype(BF16)
        spread[:tokens, b * 2 * LANES : (b + 1) * 2 * LANES] = both[:, : 2 * LANES]
        spread[tokens:, b * 2 * LANES : (b + 1) * 2 * LANES] = both[:, 2 * LANES :]
    tail = blocks[:, :, features:].astype(F32).reshape(tokens, 2 * LANES)
    tail_lane = lax.broadcasted_iota(jnp.int32, tail.shape, 1)
    mine = jnp.sum(
        jnp.where((tail_lane == me) | (tail_lane == me + LANES), tail, 0.0), axis=1, keepdims=True
    )

    def project(p, carry):
        weights = jnp.concatenate(
            [
                wide_v.at[2 * p].reshape(2 * features, LANES)[...],
                wide_v.at[2 * p + 1].reshape(2 * features, LANES)[...],
            ],
            axis=1,
        )
        projected = jnp.dot(spread[...], weights, preferred_element_type=F32)
        gate, up = projected[:tokens], projected[tokens:]
        hidden_v[p] = (gate / (1.0 + jnp.exp(-gate)) * up).astype(BF16)
        return carry

    lax.fori_loop(0, strips // 2, project, 0)
    down_copy.wait()
    hidden = jnp.concatenate([hidden_v[p] for p in range(strips // 2)], axis=1)
    step = 512
    for b in range(features // step):
        span = slice(b * step, (b + 1) * step)
        value = jnp.dot(hidden, down_v[:, span], preferred_element_type=F32) * mine
        value = value.reshape(n, rows, step)
        partial_v[:, :, span] = value
        out_blocks[:, :, span] = value.astype(BF16)

    sums = []

    def send_sum(src, dst, send_index, recv_index, peer):
        copy = remote(src, dst, sum_send.at[send_index], sum_recv.at[recv_index], peer)
        copy.start()
        sums.append(copy)

    def await_sum(dst, index):
        remote(dst, dst, sum_send.at[0], sum_recv.at[index], sibling).wait_recv()

    order = list(range(1, depth)) + [0]
    lines = [lax.rem(z + d, depth) for d in order]
    for line in lines:
        for side in (1 - y, y):
            send_sum(
                out_blocks.at[line * 4 + side * 2 + (1 - c)], core_in.at[line * 2 + side],
                len(sums), line * 2 + side, sibling,
            )
    for line in lines:
        await_sum(core_in.at[line * 2 + (1 - y)], line * 2 + (1 - y))
        value = partial_v[line * 4 + (1 - y) * 2 + c] + core_in[line * 2 + (1 - y)].astype(F32)
        side_out[line] = value.astype(BF16)
        send_sum(side_out.at[line], side_in.at[line], len(sums), 2 * depth + line, across)
        await_sum(core_in.at[line * 2 + y], line * 2 + y)
        partial_v[line * 4 + y * 2 + c] += core_in[line * 2 + y].astype(F32)
    for line in lines:
        await_sum(side_in.at[line], 2 * depth + line)
        value = partial_v[line * 4 + y * 2 + c] + side_in[line].astype(F32)
        if line is lines[-1]:
            residual_v[...] += value
        else:
            far_out[line] = value.astype(BF16)
            send_sum(
                far_out.at[line], far_in.at[z], len(sums), 3 * depth + z, line * 4 + y * 2 + c
            )
    for line in lines[:-1]:
        await_sum(far_in.at[line], 3 * depth + line)
        residual_v[...] += far_in[line].astype(F32)
    mixed_ref[...] = residual_v[...].astype(BF16)

    def sent_prev(step, carry):
        prev_copy(step).wait_send()
        return carry

    lax.fori_loop(1, n, sent_prev, 0)
    for copy in started + sums:
        copy.wait_send()
    attended_copy.wait()


def fused_shards(
    resid,
    prev_rows,
    prev_slots,
    prev_gates,
    query,
    cache,
    lengths,
    norm_gain,
    router,
    slot_expert,
    expert_ids,
    gate_up,
    down,
):
    n = lax.axis_size("node")
    rows, features = resid.shape
    capacity = prev_rows.shape[3]
    units = down.shape[1]
    strips = units // LANES
    depth = n // 4
    tokens = n * rows
    smem = pl.BlockSpec(memory_space=pltpu.SMEM)
    vmem = pl.BlockSpec(memory_space=pltpu.VMEM)
    anywhere = pl.BlockSpec(memory_space=pl.ANY)
    block = (rows, features)
    dma = pltpu.SemaphoreType.DMA
    attended_shape = query.shape[:2] + (LATENT,)
    return pl.pallas_call(
        functools.partial(fused_kernel, n),
        out_shape=(
            jax.ShapeDtypeStruct(attended_shape, BF16),
            jax.ShapeDtypeStruct(block, BF16),
        ),
        in_specs=[smem, smem] + [vmem] * 6 + [anywhere] * 5,
        out_specs=(anywhere, vmem),
        scratch_shapes=[
            pltpu.VMEM((n, capacity, features), BF16),
            pltpu.VMEM((n * capacity, features), F32),
            pltpu.VMEM(query.shape, BF16),
            pltpu.VMEM(cache.shape, BF16),
            pltpu.VMEM(attended_shape, BF16),
            pltpu.VMEM((strips, features, 2, LANES), BF16),
            pltpu.VMEM((units, features), BF16),
            pltpu.VMEM((n, rows, features + 2 * LANES), BF16),
            pltpu.VMEM((2 * tokens, 2 * features), BF16),
            pltpu.VMEM((strips // 2, tokens, 2 * LANES), BF16),
            pltpu.VMEM((n,) + block, F32),
            pltpu.VMEM((n,) + block, BF16),
            pltpu.VMEM((2 * depth,) + block, BF16),
            pltpu.VMEM((depth,) + block, BF16),
            pltpu.VMEM((depth,) + block, BF16),
            pltpu.VMEM((depth,) + block, BF16),
            pltpu.VMEM((depth,) + block, BF16),
            pltpu.VMEM(block, F32),
            dma((5,)),
            dma((strips,)),
            dma((n,)),
            dma((n,)),
            dma((n,)),
            dma((n,)),
            dma((n,)),
            dma((n,)),
        ],
        compiler_params=pltpu.CompilerParams(
            collective_id=0, has_side_effects=True, vmem_limit_bytes=56 * 2**20
        ),
        name="fused_step",
    )(
        lengths,
        slot_expert,
        resid,
        prev_slots.T,
        prev_gates.T,
        norm_gain.reshape(1, features),
        router.T,
        expert_ids.T,
        prev_rows,
        query,
        cache,
        gate_up,
        down,
    )


def solution(mesh):
    fused = mesh.shape["local"] == 1 and mesh.shape["node"] % 4 == 0
    return jax.shard_map(
        fused_shards if fused else shards,
        mesh=mesh,
        in_specs=(
            P(("groups", "node", "local"), None),
            P(("groups", "node"), "local", None, None, None),
            P(("groups", "node", "local"), None),
            P(("groups", "node", "local"), None),
            P(("groups", "node", "local"), None, None),
            P(("groups", "node", "local"), None, None),
            P(("groups", "node", "local")),
            P(),
            P(),
            P(),
            P(("groups", "node", "local"), None),
            P("node", None, None, "local"),
            P("node", "local", None),
        ),
        out_specs=(
            P(("groups", "node", "local"), None, None),
            P(("groups", "node", "local"), None),
        ),
        check_vma=False,
    )
```

```python
import functools

import jax
import jax.numpy as jnp
from jax import lax
from jax.experimental import pallas as pl
from jax.experimental.pallas import tpu as pltpu
from jax.sharding import PartitionSpec as P

LATENT = 512
ROPE = 64
NOPE = 128


def slot_places(targets):
    pair_count = targets.shape[0]
    same_slot = (targets[:, None] == targets[None, :]).astype(jnp.int32)
    earlier = (jnp.arange(pair_count)[None, :] < jnp.arange(pair_count)[:, None]).astype(jnp.int32)
    return jnp.sum(same_slot * earlier, axis=1)


def selector(targets, places, slot_count, capacity):
    column = jnp.arange(slot_count * capacity, dtype=jnp.int32)[None, :]
    return (column == (targets * capacity + places)[:, None]).astype(jnp.bfloat16)


def expert_partial(gathered, gate_up, down):
    features = gathered.shape[-1]
    unit_count = down.shape[1]
    flat_rows = gathered.reshape(-1, features)
    projected = jnp.dot(
        flat_rows, gate_up.reshape(features, 2 * unit_count), preferred_element_type=jnp.float32
    )
    hidden = (jax.nn.silu(projected[:, :unit_count]) * projected[:, unit_count:]).astype(
        jnp.bfloat16
    )
    partial_value = jnp.dot(
        hidden, down.reshape(unit_count, features), preferred_element_type=jnp.float32
    )
    return partial_value.reshape(gathered.shape)


def shards(
    resid,
    prev_rows,
    prev_slots,
    prev_gates,
    query,
    cache,
    lengths,
    norm_gain,
    router,
    slot_expert,
    expert_ids,
    gate_up,
    down,
):
    slot_count = lax.axis_size("node")
    core_count = lax.axis_size("local")
    row_count, features = resid.shape
    top_k = expert_ids.shape[1]
    pair_count = row_count * top_k
    capacity = prev_rows.shape[3]
    returned = lax.all_to_all(
        prev_rows.reshape(slot_count, capacity, features),
        "node",
        split_axis=0,
        concat_axis=0,
        tiled=True,
    )
    prev_targets = prev_slots.reshape(pair_count)
    prev_pick = selector(prev_targets, slot_places(prev_targets), slot_count, capacity)
    values = jnp.dot(
        prev_pick,
        returned.reshape(slot_count * capacity, features),
        preferred_element_type=jnp.float32,
    )
    values = values.reshape(row_count, top_k, features)
    residual = resid.astype(jnp.float32) + jnp.sum(prev_gates[:, :, None] * values, axis=1)
    mean_square = jnp.mean(residual * residual, axis=1, keepdims=True)
    normed = (residual * lax.rsqrt(mean_square + 1e-06) * norm_gain[None, :]).astype(jnp.bfloat16)
    logits = jnp.dot(normed, router, preferred_element_type=jnp.float32)
    expert_count = router.shape[1]
    chosen = expert_ids[:, :, None] == jnp.arange(expert_count, dtype=jnp.int32)[None, None, :]
    picked = jnp.sum(jnp.where(chosen, logits[:, None, :], 0.0), axis=2)
    score = jax.nn.sigmoid(picked)
    gate_weight = 2.5 * score / jnp.sum(score, axis=1, keepdims=True)
    flat_ids = expert_ids.reshape(pair_count)
    holds_it = slot_expert[None, :] == flat_ids[:, None]
    slot_index = jnp.arange(slot_count, dtype=jnp.int32)[None, :]
    targets = jnp.min(jnp.where(holds_it, slot_index, slot_count), axis=1)
    pick = selector(targets, slot_places(targets), slot_count, capacity)
    repeated = jnp.broadcast_to(normed[:, None, :], (row_count, top_k, features)).reshape(
        pair_count, features
    )
    outgoing = jnp.einsum("pk,pd->kd", pick, repeated, preferred_element_type=jnp.float32).astype(
        jnp.bfloat16
    )
    outgoing = outgoing.reshape(slot_count, capacity, features)
    doubled = jnp.broadcast_to(outgoing[:, None], (slot_count, core_count, capacity, features))
    doubled = doubled.reshape(slot_count * core_count, capacity, features)
    arrived = lax.all_to_all(doubled, ("node", "local"), split_axis=0, concat_axis=0, tiled=True)
    gathered = arrived.reshape(slot_count, core_count, capacity, features)
    partial_value = expert_partial(gathered, gate_up, down)
    summed = lax.psum_scatter(partial_value, "local", scatter_dimension=1, tiled=True)
    expert_out = summed.astype(jnp.bfloat16).reshape(slot_count, capacity, features)
    came_back = lax.all_to_all(expert_out, "node", split_axis=0, concat_axis=0, tiled=True)
    outputs = jnp.dot(
        pick, came_back.reshape(slot_count * capacity, features), preferred_element_type=jnp.float32
    )
    outputs = outputs.reshape(row_count, top_k, features)
    routed = jnp.sum(gate_weight[:, :, None] * outputs, axis=1)
    mixed_out = (residual + routed).astype(jnp.bfloat16)
    score_scale = (NOPE + ROPE) ** (-0.5)
    scores = (
        jnp.einsum("thc,tlc->thl", query, cache, preferred_element_type=jnp.float32) * score_scale
    )
    positions = cache.shape[1]
    in_range = jnp.arange(positions)[None, None, :] < lengths[:, None, None]
    scores = jnp.where(in_range, scores, -1e30)
    row_max = jnp.max(scores, axis=2, keepdims=True)
    expo = jnp.where(in_range, jnp.exp(scores - row_max), 0.0)
    weights = (expo / jnp.sum(expo, axis=2, keepdims=True)).astype(jnp.bfloat16)
    attended = jnp.einsum(
        "thl,tlc->thc", weights, cache[:, :, :LATENT], preferred_element_type=jnp.float32
    )
    return (attended.astype(jnp.bfloat16), mixed_out)


LANES = 128
MESH = pl.DeviceIdType.MESH
F32 = jnp.float32
BF16 = jnp.bfloat16


def remote(src, dst, send_sem, recv_sem, peer):
    return pltpu.make_async_remote_copy(
        src_ref=src,
        dst_ref=dst,
        send_sem=send_sem,
        recv_sem=recv_sem,
        device_id={"node": peer},
        device_id_type=MESH,
    )


def columns_of(ref):
    top_k, rows = ref.shape
    values = ref[...].astype(F32)
    diagonal = lax.broadcasted_iota(jnp.int32, (rows, rows), 0) == lax.broadcasted_iota(
        jnp.int32, (rows, rows), 1
    )
    return [
        jnp.sum(
            jnp.where(diagonal, jnp.broadcast_to(values[k : k + 1, :], (rows, rows)), 0.0),
            axis=1,
            keepdims=True,
        )
        for k in range(top_k)
    ]


def fused_kernel(
    n,
    lengths_ref,
    slot_expert_ref,
    resid_ref,
    slots_ref,
    gates_ref,
    gain_ref,
    router_ref,
    ids_ref,
    prev_hbm,
    query_hbm,
    cache_hbm,
    gate_up_hbm,
    down_hbm,
    attended_hbm,
    mixed_ref,
    prev_in,
    prev_f32,
    query_v,
    cache_v,
    attended_v,
    wide_v,
    down_v,
    blocks,
    gate_v,
    up_v,
    tokens_v,
    hidden_v,
    partial_v,
    out_blocks,
    core_in,
    side_out,
    side_in,
    far_out,
    far_in,
    residual_v,
    local_sem,
    wide_sem,
    prev_send,
    prev_recv,
    gather_send,
    gather_recv,
    sum_send,
    sum_recv,
):
    me = lax.axis_index("node")
    depth = n // 4
    z, y, c = me // 4, (me // 2) % 2, me % 2
    rows, features = resid_ref.shape
    capacity = prev_hbm.shape[3]
    units = down_v.shape[0]
    strips = units // LANES

    query_copy = pltpu.make_async_copy(query_hbm, query_v, local_sem.at[0])
    cache_copy = pltpu.make_async_copy(cache_hbm, cache_v, local_sem.at[1])
    down_copy = pltpu.make_async_copy(down_hbm.at[0], down_v, local_sem.at[2])
    own_prev = pltpu.make_async_copy(prev_hbm.at[0, 0, me], prev_in.at[me], local_sem.at[3])

    def strip_copy(i):
        return pltpu.make_async_copy(
            gate_up_hbm.at[0, :, :, pl.ds(i * LANES, LANES)], wide_v.at[i], wide_sem.at[i]
        )

    query_copy.start()
    cache_copy.start()
    own_prev.start()

    barrier = pltpu.get_barrier_semaphore()

    def greet(step, carry):
        pl.semaphore_signal(
            barrier, inc=1, device_id={"node": lax.rem(me + step, n)}, device_id_type=MESH
        )
        return carry

    lax.fori_loop(1, n, greet, 0)
    pl.semaphore_wait(barrier, n - 1)

    def prev_copy(step):
        peer = lax.rem(me + step, n)
        return remote(
            prev_hbm.at[0, 0, peer], prev_in.at[me], prev_send.at[step], prev_recv.at[me], peer
        )

    def send_prev(step, carry):
        prev_copy(step).start()
        return carry

    lax.fori_loop(1, n, send_prev, 0)
    for i in range(strips):
        strip_copy(i).start()
    down_copy.start()

    query_copy.wait()
    cache_copy.wait()
    positions = cache_v.shape[1]
    heads = query_v.shape[1]

    def attend(r, carry):
        keys = cache_v[r]
        scores = lax.dot_general(
            query_v[r], keys, (((1,), (1,)), ((), ())), preferred_element_type=F32
        ) * ((NOPE + ROPE) ** (-0.5))
        live = lax.broadcasted_iota(jnp.int32, (heads, positions), 1) < lengths_ref[r]
        scores = jnp.where(live, scores, -1e30)
        row_max = jnp.max(scores, axis=1, keepdims=True)
        expo = jnp.where(live, jnp.exp(scores - row_max), 0.0)
        weights = (expo / jnp.sum(expo, axis=1, keepdims=True)).astype(BF16)
        attended_v[r] = jnp.dot(
            weights, keys[:, :LATENT], preferred_element_type=F32
        ).astype(BF16)
        return carry

    lax.fori_loop(0, query_v.shape[0], attend, 0)
    attended_copy = pltpu.make_async_copy(attended_v, attended_hbm, local_sem.at[4])
    attended_copy.start()

    width = n * capacity
    lane = lax.broadcasted_iota(jnp.int32, (rows, width), 1)
    lane_slot = (lane // capacity).astype(F32)
    lane_place = (lane % capacity).astype(F32)
    uses = jnp.zeros((rows, width), F32)
    gate_row = jnp.zeros((rows, width), F32)
    for slot, gate in zip(columns_of(slots_ref), columns_of(gates_ref)):
        hit = lane_slot == slot
        uses = uses + jnp.where(hit, 1.0, 0.0)
        gate_row = gate_row + jnp.where(hit, gate, 0.0)
    token = lax.broadcasted_iota(jnp.int32, (rows, width), 0)
    places = jnp.zeros((rows, width), F32)
    for t in range(rows - 1):
        places = places + jnp.where(token > t, uses[t : t + 1, :], 0.0)
    gate_row = jnp.where(places == lane_place, gate_row, 0.0)
    gate_high = gate_row.astype(BF16)
    rest = gate_row - gate_high.astype(F32)
    gate_mid = rest.astype(BF16)
    gate_low = (rest - gate_mid.astype(F32)).astype(BF16)

    slot_lane = lax.broadcasted_iota(jnp.int32, (1, LANES), 1)
    half = LANES // 2
    held = jnp.full((1, LANES), -1, jnp.int32)
    for i in range(n):
        held = jnp.where(slot_lane % half == i, slot_expert_ref[i], held)
    first = jnp.ones((1, LANES), F32)
    for i in range(n):
        first = jnp.where((held == slot_expert_ref[i]) & (slot_lane % half > i), 0.0, first)
    held = held.astype(F32)

    row = lax.broadcasted_iota(jnp.int32, (2 * LANES, 2 * LANES), 0)
    column = lax.broadcasted_iota(jnp.int32, (2 * LANES, 2 * LANES), 1)
    parting = jnp.where(
        ((row < LANES) & (column == 2 * row))
        | ((row >= LANES) & (column == 2 * (row - LANES) + 1)),
        1.0,
        0.0,
    ).astype(BF16)
    for p in range(strips // 2):
        strip_copy(2 * p).wait()
        strip_copy(2 * p + 1).wait()
        left, right = (wide_v.at[2 * p + i].reshape(2 * features, LANES) for i in range(2))
        for b in range(features // LANES):
            span = slice(b * 2 * LANES, (b + 1) * 2 * LANES)
            mixed = jnp.concatenate([left[span, :], right[span, :]], axis=1)
            apart = jnp.dot(parting, mixed, preferred_element_type=F32).astype(BF16)
            rows_of = slice(b * LANES, (b + 1) * LANES)
            gate_v[rows_of, p * 2 * LANES : (p + 1) * 2 * LANES] = apart[:LANES]
            up_v[rows_of, p * 2 * LANES : (p + 1) * 2 * LANES] = apart[LANES:]

    own_prev.wait()

    def take_prev(step, carry):
        source = lax.rem(me + step, n)
        remote(
            prev_hbm.at[0, 0, me], prev_in.at[source], prev_send.at[step], prev_recv.at[source],
            source,
        ).wait_recv()
        return carry

    lax.fori_loop(1, n, take_prev, 0)
    for i in range(n):
        prev_f32[i * capacity : (i + 1) * capacity, :] = prev_in[i].astype(F32)
    prev_rows = prev_f32[...].astype(BF16)
    combined = (
        jnp.dot(gate_high, prev_rows, preferred_element_type=F32)
        + jnp.dot(gate_mid, prev_rows, preferred_element_type=F32)
        + jnp.dot(gate_low, prev_rows, preferred_element_type=F32)
    )
    residual = resid_ref[...].astype(F32) + combined
    residual_v[...] = residual
    mean_square = jnp.sum(residual * residual, axis=1, keepdims=True) * (1.0 / features)
    normed = (residual * lax.rsqrt(mean_square + 1e-06) * gain_ref[...].reshape(1, features)).astype(BF16)
    logits = lax.dot_general(
        normed, router_ref[...], (((1,), (1,)), ((), ())), preferred_element_type=F32
    )
    expert_lane = lax.broadcasted_iota(jnp.int32, logits.shape, 1).astype(F32)
    ids = columns_of(ids_ref)
    picked = [
        jnp.sum(jnp.where(expert_lane == chosen, logits, 0.0), axis=1, keepdims=True)
        for chosen in ids
    ]
    score = [1.0 / (1.0 + jnp.exp(-value)) for value in picked]
    total = functools.reduce(lambda a, b: a + b, score)
    slot_weight = jnp.zeros((rows, LANES), F32)
    for chosen, value in zip(ids, score):
        slot_weight = slot_weight + jnp.where(held == chosen, 2.5 * value / total, 0.0)
    slot_weight = slot_weight * first
    weight_high = slot_weight.astype(BF16)
    weight_low = (slot_weight - weight_high.astype(F32)).astype(BF16)
    blocks[me, :, :features] = normed
    blocks[me, :, features:] = jnp.where(
        lax.broadcasted_iota(jnp.int32, slot_weight.shape, 1) < half,
        weight_high.astype(F32),
        weight_low.astype(F32),
    ).astype(BF16)

    across, sibling = z * 4 + (1 - y) * 2 + c, z * 4 + y * 2 + (1 - c)
    started = []

    def index_of(line):
        return line * 4 + y * 2 + c

    def block_copy(index, send_index, peer):
        return remote(
            blocks.at[index], blocks.at[index], gather_send.at[send_index],
            gather_recv.at[index], peer,
        )

    def send_block(index, peer):
        copy = block_copy(index, len(started), peer)
        copy.start()
        started.append(copy)

    def await_block(index):
        block_copy(index, 0, sibling).wait_recv()

    def line_copy(way, d):
        return block_copy(index_of(z - way * d), n + (1 + way) * depth // 2 + d, index_of(z + way))

    def passes_on(way, d):
        source, target = z - way * d, z + way
        return (source >= 0) & (source < depth) & (target >= 0) & (target < depth)

    for way in (1, -1):
        pl.when(passes_on(way, 0))(line_copy(way, 0).start)
    send_block(me, across)
    send_block(me, sibling)
    for d in range(1, depth):
        for way in (1, -1):
            source = z - way * d

            @pl.when((source >= 0) & (source < depth))
            def _():
                await_block(index_of(source))
                pl.when(passes_on(way, d))(line_copy(way, d).start)
                side = block_copy(index_of(source), 2 + source, across)
                side.start()
                near = block_copy(index_of(source), 2 + depth + source, sibling)
                near.start()
        if d == 1:
            await_block(across)
            block_copy(across, 2 + 2 * depth, sibling).start()
    for d in range(1, depth):
        for way in (1, -1):
            source = z - way * d

            @pl.when((source >= 0) & (source < depth))
            def _():
                other = source * 4 + (1 - y) * 2 + c
                await_block(other)
                block_copy(other, 3 + 2 * depth + source, sibling).start()
    for d in range(depth):
        for side in range(2):
            await_block(lax.rem(z + d, depth) * 4 + side * 2 + (1 - c))

    tokens = n * rows
    for b in range(features // LANES):
        span = slice(b * LANES, (b + 1) * LANES)
        tokens_v[:, span] = blocks[:, :, span].astype(F32).reshape(tokens, LANES).astype(BF16)
    tail = blocks[:, :, features:].astype(F32).reshape(tokens, LANES)
    tail_lane = lax.broadcasted_iota(jnp.int32, tail.shape, 1)
    mine = jnp.sum(
        jnp.where((tail_lane == me) | (tail_lane == me + half), tail, 0.0), axis=1, keepdims=True
    )
    for p in range(strips // 2):
        span = slice(p * 2 * LANES, (p + 1) * 2 * LANES)
        gate = jnp.dot(tokens_v[...], gate_v[:, span], preferred_element_type=F32)
        up = jnp.dot(tokens_v[...], up_v[:, span], preferred_element_type=F32)
        hidden_v[p] = (gate / (1.0 + jnp.exp(-gate)) * up).astype(BF16)
    down_copy.wait()
    hidden = jnp.concatenate([hidden_v[p] for p in range(strips // 2)], axis=1)
    step = 512
    for b in range(features // step):
        span = slice(b * step, (b + 1) * step)
        value = jnp.dot(hidden, down_v[:, span], preferred_element_type=F32) * mine
        value = value.reshape(n, rows, step)
        partial_v[:, :, span] = value
        out_blocks[:, :, span] = value.astype(BF16)

    sums = []

    def send_sum(src, dst, send_index, recv_index, peer):
        copy = remote(src, dst, sum_send.at[send_index], sum_recv.at[recv_index], peer)
        copy.start()
        sums.append(copy)

    def await_sum(dst, index):
        remote(dst, dst, sum_send.at[0], sum_recv.at[index], sibling).wait_recv()

    lines = []
    for d in range(depth // 2):
        lines += [depth - 1 - d, d]
    for line in lines:
        for side in (1 - y, y):
            send_sum(
                out_blocks.at[line * 4 + side * 2 + (1 - c)], core_in.at[line * 2 + side],
                len(sums), line * 2 + side, sibling,
            )
    for line in lines:
        await_sum(core_in.at[line * 2 + (1 - y)], line * 2 + (1 - y))
        value = partial_v[line * 4 + (1 - y) * 2 + c] + core_in[line * 2 + (1 - y)].astype(F32)
        side_out[line] = value.astype(BF16)
        send_sum(side_out.at[line], side_in.at[line], len(sums), 2 * depth + line, across)
        await_sum(core_in.at[line * 2 + y], line * 2 + y)
        partial_v[line * 4 + y * 2 + c] += core_in[line * 2 + y].astype(F32)

    def far_copy(way, line):
        return remote(
            far_out.at[line], far_in.at[(1 + way) // 2, line], sum_send.at[3 * depth + line],
            sum_recv.at[(4 - way) * depth + line], index_of(z + way),
        )

    def take_far(way, line):
        far_copy(way, line).wait_recv()
        partial_v[index_of(line)] += far_in[(1 + way) // 2, line].astype(F32)

    for line in lines:
        await_sum(side_in.at[line], 2 * depth + line)
        partial_v[index_of(line)] += side_in[line].astype(F32)

        @pl.when(z < line)
        def _():
            pl.when(z > 0)(lambda: take_far(1, line))
            far_out[line] = partial_v[index_of(line)].astype(BF16)
            far_copy(1, line).start()

        @pl.when(z > line)
        def _():
            pl.when(z < depth - 1)(lambda: take_far(-1, line))
            far_out[line] = partial_v[index_of(line)].astype(BF16)
            far_copy(-1, line).start()

    for line in range(depth):
        @pl.when(z == line)
        def _():
            if line > 0:
                take_far(1, line)
            if line < depth - 1:
                take_far(-1, line)

    mixed_ref[...] = residual_v[...] + partial_v[me]

    for line in range(depth):
        pl.when(z < line)(lambda: far_copy(1, line).wait_send())
        pl.when(z > line)(lambda: far_copy(-1, line).wait_send())
    for d in range(depth):
        for way in (1, -1):
            pl.when(passes_on(way, d))(lambda: line_copy(way, d).wait_send())
    block_copy(across, 2 + 2 * depth, sibling).wait_send()
    for d in range(1, depth):
        source = lax.rem(z + d, depth)
        other = source * 4 + (1 - y) * 2 + c
        block_copy(index_of(source), 2 + source, across).wait_send()
        block_copy(index_of(source), 2 + depth + source, sibling).wait_send()
        block_copy(other, 3 + 2 * depth + source, sibling).wait_send()

    def sent_prev(step, carry):
        prev_copy(step).wait_send()
        return carry

    lax.fori_loop(1, n, sent_prev, 0)
    for copy in started + sums:
        copy.wait_send()
    attended_copy.wait()


def fused_shards(
    resid,
    prev_rows,
    prev_slots,
    prev_gates,
    query,
    cache,
    lengths,
    norm_gain,
    router,
    slot_expert,
    expert_ids,
    gate_up,
    down,
):
    n = lax.axis_size("node")
    rows, features = resid.shape
    capacity = prev_rows.shape[3]
    units = down.shape[1]
    strips = units // LANES
    depth = n // 4
    tokens = n * rows
    smem = pl.BlockSpec(memory_space=pltpu.SMEM)
    vmem = pl.BlockSpec(memory_space=pltpu.VMEM)
    anywhere = pl.BlockSpec(memory_space=pl.ANY)
    block = (rows, features)
    dma = pltpu.SemaphoreType.DMA
    attended_shape = query.shape[:2] + (LATENT,)
    attended, mixed = pl.pallas_call(
        functools.partial(fused_kernel, n),
        out_shape=(
            jax.ShapeDtypeStruct(attended_shape, BF16),
            jax.ShapeDtypeStruct(block, F32),
        ),
        in_specs=[smem, smem] + [vmem] * 6 + [anywhere] * 5,
        out_specs=(anywhere, vmem),
        scratch_shapes=[
            pltpu.VMEM((n, capacity, features), BF16),
            pltpu.VMEM((n * capacity, features), F32),
            pltpu.VMEM(query.shape, BF16),
            pltpu.VMEM(cache.shape, BF16),
            pltpu.VMEM(attended_shape, BF16),
            pltpu.VMEM((strips, features, 2, LANES), BF16),
            pltpu.VMEM((units, features), BF16),
            pltpu.VMEM((n, rows, features + LANES), BF16),
            pltpu.VMEM((features, units), BF16),
            pltpu.VMEM((features, units), BF16),
            pltpu.VMEM((tokens, features), BF16),
            pltpu.VMEM((strips // 2, tokens, 2 * LANES), BF16),
            pltpu.VMEM((n,) + block, F32),
            pltpu.VMEM((n,) + block, BF16),
            pltpu.VMEM((2 * depth,) + block, BF16),
            pltpu.VMEM((depth,) + block, BF16),
            pltpu.VMEM((depth,) + block, BF16),
            pltpu.VMEM((depth,) + block, BF16),
            pltpu.VMEM((2, depth) + block, BF16),
            pltpu.VMEM(block, F32),
            dma((5,)),
            dma((strips,)),
            dma((n,)),
            dma((n,)),
            dma((2 * n,)),
            dma((n,)),
            dma((n,)),
            dma((2 * n,)),
        ],
        compiler_params=pltpu.CompilerParams(
            collective_id=0, has_side_effects=True, vmem_limit_bytes=58 * 2**20
        ),
        name="fused_step",
    )(
        lengths,
        slot_expert,
        resid,
        prev_slots.T,
        prev_gates.T,
        norm_gain,
        router.T,
        expert_ids.T,
        prev_rows,
        query,
        cache,
        gate_up,
        down,
    )
    return attended, mixed.astype(BF16)


def solution(mesh):
    fused = mesh.shape["local"] == 1 and mesh.shape["node"] % 4 == 0
    return jax.shard_map(
        fused_shards if fused else shards,
        mesh=mesh,
        in_specs=(
            P(("groups", "node", "local"), None),
            P(("groups", "node"), "local", None, None, None),
            P(("groups", "node", "local"), None),
            P(("groups", "node", "local"), None),
            P(("groups", "node", "local"), None, None),
            P(("groups", "node", "local"), None, None),
            P(("groups", "node", "local")),
            P(),
            P(),
            P(),
            P(("groups", "node", "local"), None),
            P("node", None, None, "local"),
            P("node", "local", None),
        ),
        out_specs=(
            P(("groups", "node", "local"), None, None),
            P(("groups", "node", "local"), None),
        ),
        check_vma=False,
    )
```

```python
import functools

import jax
import jax.numpy as jnp
from jax import lax
from jax.experimental import pallas as pl
from jax.experimental.pallas import tpu as pltpu
from jax.sharding import PartitionSpec as P

LATENT = 512
ROPE = 64
NOPE = 128


def slot_places(targets):
    pair_count = targets.shape[0]
    same_slot = (targets[:, None] == targets[None, :]).astype(jnp.int32)
    earlier = (jnp.arange(pair_count)[None, :] < jnp.arange(pair_count)[:, None]).astype(jnp.int32)
    return jnp.sum(same_slot * earlier, axis=1)


def selector(targets, places, slot_count, capacity):
    column = jnp.arange(slot_count * capacity, dtype=jnp.int32)[None, :]
    return (column == (targets * capacity + places)[:, None]).astype(jnp.bfloat16)


def expert_partial(gathered, gate_up, down):
    features = gathered.shape[-1]
    unit_count = down.shape[1]
    flat_rows = gathered.reshape(-1, features)
    projected = jnp.dot(
        flat_rows, gate_up.reshape(features, 2 * unit_count), preferred_element_type=jnp.float32
    )
    hidden = (jax.nn.silu(projected[:, :unit_count]) * projected[:, unit_count:]).astype(
        jnp.bfloat16
    )
    partial_value = jnp.dot(
        hidden, down.reshape(unit_count, features), preferred_element_type=jnp.float32
    )
    return partial_value.reshape(gathered.shape)


def shards(
    resid,
    prev_rows,
    prev_slots,
    prev_gates,
    query,
    cache,
    lengths,
    norm_gain,
    router,
    slot_expert,
    expert_ids,
    gate_up,
    down,
):
    slot_count = lax.axis_size("node")
    core_count = lax.axis_size("local")
    row_count, features = resid.shape
    top_k = expert_ids.shape[1]
    pair_count = row_count * top_k
    capacity = prev_rows.shape[3]
    returned = lax.all_to_all(
        prev_rows.reshape(slot_count, capacity, features),
        "node",
        split_axis=0,
        concat_axis=0,
        tiled=True,
    )
    prev_targets = prev_slots.reshape(pair_count)
    prev_pick = selector(prev_targets, slot_places(prev_targets), slot_count, capacity)
    values = jnp.dot(
        prev_pick,
        returned.reshape(slot_count * capacity, features),
        preferred_element_type=jnp.float32,
    )
    values = values.reshape(row_count, top_k, features)
    residual = resid.astype(jnp.float32) + jnp.sum(prev_gates[:, :, None] * values, axis=1)
    mean_square = jnp.mean(residual * residual, axis=1, keepdims=True)
    normed = (residual * lax.rsqrt(mean_square + 1e-06) * norm_gain[None, :]).astype(jnp.bfloat16)
    logits = jnp.dot(normed, router, preferred_element_type=jnp.float32)
    expert_count = router.shape[1]
    chosen = expert_ids[:, :, None] == jnp.arange(expert_count, dtype=jnp.int32)[None, None, :]
    picked = jnp.sum(jnp.where(chosen, logits[:, None, :], 0.0), axis=2)
    score = jax.nn.sigmoid(picked)
    gate_weight = 2.5 * score / jnp.sum(score, axis=1, keepdims=True)
    flat_ids = expert_ids.reshape(pair_count)
    holds_it = slot_expert[None, :] == flat_ids[:, None]
    slot_index = jnp.arange(slot_count, dtype=jnp.int32)[None, :]
    targets = jnp.min(jnp.where(holds_it, slot_index, slot_count), axis=1)
    pick = selector(targets, slot_places(targets), slot_count, capacity)
    repeated = jnp.broadcast_to(normed[:, None, :], (row_count, top_k, features)).reshape(
        pair_count, features
    )
    outgoing = jnp.einsum("pk,pd->kd", pick, repeated, preferred_element_type=jnp.float32).astype(
        jnp.bfloat16
    )
    outgoing = outgoing.reshape(slot_count, capacity, features)
    doubled = jnp.broadcast_to(outgoing[:, None], (slot_count, core_count, capacity, features))
    doubled = doubled.reshape(slot_count * core_count, capacity, features)
    arrived = lax.all_to_all(doubled, ("node", "local"), split_axis=0, concat_axis=0, tiled=True)
    gathered = arrived.reshape(slot_count, core_count, capacity, features)
    partial_value = expert_partial(gathered, gate_up, down)
    summed = lax.psum_scatter(partial_value, "local", scatter_dimension=1, tiled=True)
    expert_out = summed.astype(jnp.bfloat16).reshape(slot_count, capacity, features)
    came_back = lax.all_to_all(expert_out, "node", split_axis=0, concat_axis=0, tiled=True)
    outputs = jnp.dot(
        pick, came_back.reshape(slot_count * capacity, features), preferred_element_type=jnp.float32
    )
    outputs = outputs.reshape(row_count, top_k, features)
    routed = jnp.sum(gate_weight[:, :, None] * outputs, axis=1)
    mixed_out = (residual + routed).astype(jnp.bfloat16)
    score_scale = (NOPE + ROPE) ** (-0.5)
    scores = (
        jnp.einsum("thc,tlc->thl", query, cache, preferred_element_type=jnp.float32) * score_scale
    )
    positions = cache.shape[1]
    in_range = jnp.arange(positions)[None, None, :] < lengths[:, None, None]
    scores = jnp.where(in_range, scores, -1e30)
    row_max = jnp.max(scores, axis=2, keepdims=True)
    expo = jnp.where(in_range, jnp.exp(scores - row_max), 0.0)
    weights = (expo / jnp.sum(expo, axis=2, keepdims=True)).astype(jnp.bfloat16)
    attended = jnp.einsum(
        "thl,tlc->thc", weights, cache[:, :, :LATENT], preferred_element_type=jnp.float32
    )
    return (attended.astype(jnp.bfloat16), mixed_out)


LANES = 128
MESH = pl.DeviceIdType.MESH
F32 = jnp.float32
BF16 = jnp.bfloat16


def remote(src, dst, send_sem, recv_sem, peer):
    return pltpu.make_async_remote_copy(
        src_ref=src,
        dst_ref=dst,
        send_sem=send_sem,
        recv_sem=recv_sem,
        device_id={"node": peer},
        device_id_type=MESH,
    )


def columns_of(ref):
    top_k, rows = ref.shape
    values = ref[...].astype(F32)
    diagonal = lax.broadcasted_iota(jnp.int32, (rows, rows), 0) == lax.broadcasted_iota(
        jnp.int32, (rows, rows), 1
    )
    return [
        jnp.sum(
            jnp.where(diagonal, jnp.broadcast_to(values[k : k + 1, :], (rows, rows)), 0.0),
            axis=1,
            keepdims=True,
        )
        for k in range(top_k)
    ]


def fused_kernel(
    n,
    lengths_ref,
    slot_expert_ref,
    resid_ref,
    slots_ref,
    gates_ref,
    gain_ref,
    router_ref,
    ids_ref,
    prev_hbm,
    query_hbm,
    cache_hbm,
    gate_up_hbm,
    down_hbm,
    attended_hbm,
    mixed_ref,
    prev_in,
    prev_f32,
    query_v,
    cache_v,
    attended_v,
    wide_v,
    down_v,
    blocks,
    gate_v,
    up_v,
    tokens_v,
    hidden_v,
    partial_v,
    out_blocks,
    core_in,
    side_out,
    side_in,
    far_out,
    far_in,
    residual_v,
    local_sem,
    wide_sem,
    prev_send,
    prev_recv,
    gather_send,
    gather_recv,
    sum_send,
    sum_recv,
):
    me = lax.axis_index("node")
    depth = n // 4
    z, y, c = me // 4, (me // 2) % 2, me % 2
    rows, features = resid_ref.shape
    capacity = prev_hbm.shape[3]
    units = down_v.shape[0]
    strips = units // LANES

    query_copy = pltpu.make_async_copy(query_hbm, query_v, local_sem.at[0])
    cache_copy = pltpu.make_async_copy(cache_hbm, cache_v, local_sem.at[1])
    down_copy = pltpu.make_async_copy(down_hbm.at[0], down_v, local_sem.at[2])
    own_prev = pltpu.make_async_copy(prev_hbm.at[0, 0, me], prev_in.at[me], local_sem.at[3])

    def strip_copy(i):
        return pltpu.make_async_copy(
            gate_up_hbm.at[0, :, :, pl.ds(i * LANES, LANES)], wide_v.at[i], wide_sem.at[i]
        )

    query_copy.start()
    cache_copy.start()
    own_prev.start()

    barrier = pltpu.get_barrier_semaphore()

    def greet(step, carry):
        pl.semaphore_signal(
            barrier, inc=1, device_id={"node": lax.rem(me + step, n)}, device_id_type=MESH
        )
        return carry

    lax.fori_loop(1, n, greet, 0)
    pl.semaphore_wait(barrier, n - 1)

    def prev_copy(step):
        peer = lax.rem(me + step, n)
        return remote(
            prev_hbm.at[0, 0, peer], prev_in.at[me], prev_send.at[step], prev_recv.at[me], peer
        )

    def send_prev(step, carry):
        prev_copy(step).start()
        return carry

    lax.fori_loop(1, n, send_prev, 0)
    for i in range(strips):
        strip_copy(i).start()
    down_copy.start()

    query_copy.wait()
    cache_copy.wait()
    positions = cache_v.shape[1]
    heads = query_v.shape[1]

    def attend(r, carry):
        keys = cache_v[r]
        scores = lax.dot_general(
            query_v[r], keys, (((1,), (1,)), ((), ())), preferred_element_type=F32
        ) * ((NOPE + ROPE) ** (-0.5))
        live = lax.broadcasted_iota(jnp.int32, (heads, positions), 1) < lengths_ref[r]
        scores = jnp.where(live, scores, -1e30)
        row_max = jnp.max(scores, axis=1, keepdims=True)
        expo = jnp.where(live, jnp.exp(scores - row_max), 0.0)
        weights = (expo / jnp.sum(expo, axis=1, keepdims=True)).astype(BF16)
        attended_v[r] = jnp.dot(
            weights, keys[:, :LATENT], preferred_element_type=F32
        ).astype(BF16)
        return carry

    lax.fori_loop(0, query_v.shape[0], attend, 0)
    attended_copy = pltpu.make_async_copy(attended_v, attended_hbm, local_sem.at[4])
    attended_copy.start()

    width = n * capacity
    lane = lax.broadcasted_iota(jnp.int32, (rows, width), 1)
    lane_slot = (lane // capacity).astype(F32)
    lane_place = (lane % capacity).astype(F32)
    uses = jnp.zeros((rows, width), F32)
    gate_row = jnp.zeros((rows, width), F32)
    for slot, gate in zip(columns_of(slots_ref), columns_of(gates_ref)):
        hit = lane_slot == slot
        uses = uses + jnp.where(hit, 1.0, 0.0)
        gate_row = gate_row + jnp.where(hit, gate, 0.0)
    token = lax.broadcasted_iota(jnp.int32, (rows, width), 0)
    places = jnp.zeros((rows, width), F32)
    for t in range(rows - 1):
        places = places + jnp.where(token > t, uses[t : t + 1, :], 0.0)
    gate_row = jnp.where(places == lane_place, gate_row, 0.0)
    gate_high = gate_row.astype(BF16)
    rest = gate_row - gate_high.astype(F32)
    gate_mid = rest.astype(BF16)
    gate_low = (rest - gate_mid.astype(F32)).astype(BF16)

    slot_lane = lax.broadcasted_iota(jnp.int32, (1, LANES), 1)
    half = LANES // 2
    held = jnp.full((1, LANES), -1, jnp.int32)
    for i in range(n):
        held = jnp.where(slot_lane % half == i, slot_expert_ref[i], held)
    first = jnp.ones((1, LANES), F32)
    for i in range(n):
        first = jnp.where((held == slot_expert_ref[i]) & (slot_lane % half > i), 0.0, first)
    held = held.astype(F32)

    row = lax.broadcasted_iota(jnp.int32, (2 * LANES, 2 * LANES), 0)
    column = lax.broadcasted_iota(jnp.int32, (2 * LANES, 2 * LANES), 1)
    parting = jnp.where(
        ((row < LANES) & (column == 2 * row))
        | ((row >= LANES) & (column == 2 * (row - LANES) + 1)),
        1.0,
        0.0,
    ).astype(BF16)

    def part(p):
        strip_copy(2 * p).wait()
        strip_copy(2 * p + 1).wait()
        left, right = (wide_v.at[2 * p + i].reshape(2 * features, LANES) for i in range(2))
        for b in range(features // LANES):
            span = slice(b * 2 * LANES, (b + 1) * 2 * LANES)
            mixed = jnp.concatenate([left[span, :], right[span, :]], axis=1)
            apart = jnp.dot(parting, mixed, preferred_element_type=F32).astype(BF16)
            rows_of = slice(b * LANES, (b + 1) * LANES)
            gate_v[rows_of, p * 2 * LANES : (p + 1) * 2 * LANES] = apart[:LANES]
            up_v[rows_of, p * 2 * LANES : (p + 1) * 2 * LANES] = apart[LANES:]

    for p in range(strips // 2 - 1):
        part(p)
    own_prev.wait()

    def take_prev(step, carry):
        source = lax.rem(me + step, n)
        remote(
            prev_hbm.at[0, 0, me], prev_in.at[source], prev_send.at[step], prev_recv.at[source],
            source,
        ).wait_recv()
        return carry

    lax.fori_loop(1, n, take_prev, 0)
    for i in range(n):
        prev_f32[i * capacity : (i + 1) * capacity, :] = prev_in[i].astype(F32)
    prev_rows = prev_f32[...].astype(BF16)
    combined = (
        jnp.dot(gate_high, prev_rows, preferred_element_type=F32)
        + jnp.dot(gate_mid, prev_rows, preferred_element_type=F32)
        + jnp.dot(gate_low, prev_rows, preferred_element_type=F32)
    )
    residual = resid_ref[...].astype(F32) + combined
    residual_v[...] = residual
    mean_square = jnp.sum(residual * residual, axis=1, keepdims=True) * (1.0 / features)
    normed = (residual * lax.rsqrt(mean_square + 1e-06) * gain_ref[...].reshape(1, features)).astype(BF16)
    logits = lax.dot_general(
        normed, router_ref[...], (((1,), (1,)), ((), ())), preferred_element_type=F32
    )
    expert_lane = lax.broadcasted_iota(jnp.int32, logits.shape, 1).astype(F32)
    ids = columns_of(ids_ref)
    picked = [
        jnp.sum(jnp.where(expert_lane == chosen, logits, 0.0), axis=1, keepdims=True)
        for chosen in ids
    ]
    score = [1.0 / (1.0 + jnp.exp(-value)) for value in picked]
    total = functools.reduce(lambda a, b: a + b, score)
    slot_weight = jnp.zeros((rows, LANES), F32)
    for chosen, value in zip(ids, score):
        slot_weight = slot_weight + jnp.where(held == chosen, 2.5 * value / total, 0.0)
    slot_weight = slot_weight * first
    weight_high = slot_weight.astype(BF16)
    weight_low = (slot_weight - weight_high.astype(F32)).astype(BF16)
    blocks[me, :, :features] = normed
    blocks[me, :, features:] = jnp.where(
        lax.broadcasted_iota(jnp.int32, slot_weight.shape, 1) < half,
        weight_high.astype(F32),
        weight_low.astype(F32),
    ).astype(BF16)

    across, sibling = z * 4 + (1 - y) * 2 + c, z * 4 + y * 2 + (1 - c)
    started = []

    def send_block(index, peer):
        copy = remote(
            blocks.at[index], blocks.at[index], gather_send.at[len(started)],
            gather_recv.at[index], peer,
        )
        copy.start()
        started.append(copy)

    def await_block(index):
        remote(
            blocks.at[index], blocks.at[index], gather_send.at[0], gather_recv.at[index], sibling
        ).wait_recv()

    for d in range(1, depth):
        send_block(me, lax.rem(z + d, depth) * 4 + y * 2 + c)
    send_block(me, across)
    send_block(me, sibling)
    part(strips // 2 - 1)
    await_block(across)
    send_block(across, sibling)
    for d in range(1, depth):
        other = lax.rem(z + d, depth) * 4 + y * 2 + c
        await_block(other)
        send_block(other, across)
        send_block(other, sibling)
    for d in range(1, depth):
        other = lax.rem(z + d, depth) * 4 + (1 - y) * 2 + c
        await_block(other)
        send_block(other, sibling)
    for d in range(depth):
        for side in range(2):
            await_block(lax.rem(z + d, depth) * 4 + side * 2 + (1 - c))
    tokens = n * rows
    for b in range(features // LANES):
        span = slice(b * LANES, (b + 1) * LANES)
        tokens_v[:, span] = blocks[:, :, span].astype(F32).reshape(tokens, LANES).astype(BF16)
    tail = blocks[:, :, features:].astype(F32).reshape(tokens, LANES)
    tail_lane = lax.broadcasted_iota(jnp.int32, tail.shape, 1)
    mine = jnp.sum(
        jnp.where((tail_lane == me) | (tail_lane == me + half), tail, 0.0), axis=1, keepdims=True
    )
    for p in range(strips // 2):
        span = slice(p * 2 * LANES, (p + 1) * 2 * LANES)
        gate = jnp.dot(tokens_v[...], gate_v[:, span], preferred_element_type=F32)
        up = jnp.dot(tokens_v[...], up_v[:, span], preferred_element_type=F32)
        hidden_v[p] = (gate / (1.0 + jnp.exp(-gate)) * up).astype(BF16)
    down_copy.wait()
    hidden = jnp.concatenate([hidden_v[p] for p in range(strips // 2)], axis=1)
    step = 512
    for b in range(features // step):
        span = slice(b * step, (b + 1) * step)
        value = jnp.dot(hidden, down_v[:, span], preferred_element_type=F32) * mine
        value = value.reshape(n, rows, step)
        partial_v[:, :, span] = value
        out_blocks[:, :, span] = value.astype(BF16)

    sums = []

    def send_sum(src, dst, send_index, recv_index, peer):
        copy = remote(src, dst, sum_send.at[send_index], sum_recv.at[recv_index], peer)
        copy.start()
        sums.append(copy)

    def await_sum(dst, index):
        remote(dst, dst, sum_send.at[0], sum_recv.at[index], sibling).wait_recv()

    order = list(range(1, depth)) + [0]
    lines = [lax.rem(z + d, depth) for d in order]
    for line in lines:
        for side in (1 - y, y):
            send_sum(
                out_blocks.at[line * 4 + side * 2 + (1 - c)], core_in.at[line * 2 + side],
                len(sums), line * 2 + side, sibling,
            )
    for line in lines:
        await_sum(core_in.at[line * 2 + (1 - y)], line * 2 + (1 - y))
        value = partial_v[line * 4 + (1 - y) * 2 + c] + core_in[line * 2 + (1 - y)].astype(F32)
        side_out[line] = value.astype(BF16)
        send_sum(side_out.at[line], side_in.at[line], len(sums), 2 * depth + line, across)
        await_sum(core_in.at[line * 2 + y], line * 2 + y)
        partial_v[line * 4 + y * 2 + c] += core_in[line * 2 + y].astype(F32)
    for line in lines:
        await_sum(side_in.at[line], 2 * depth + line)
        value = partial_v[line * 4 + y * 2 + c] + side_in[line].astype(F32)
        if line is lines[-1]:
            residual_v[...] += value
        else:
            far_out[line] = value.astype(BF16)
            send_sum(
                far_out.at[line], far_in.at[z], len(sums), 3 * depth + z, line * 4 + y * 2 + c
            )
    for line in lines[:-1]:
        await_sum(far_in.at[line], 3 * depth + line)
        residual_v[...] += far_in[line].astype(F32)
    mixed_ref[...] = residual_v[...]

    def sent_prev(step, carry):
        prev_copy(step).wait_send()
        return carry

    lax.fori_loop(1, n, sent_prev, 0)
    for copy in started + sums:
        copy.wait_send()
    attended_copy.wait()


def fused_shards(
    resid,
    prev_rows,
    prev_slots,
    prev_gates,
    query,
    cache,
    lengths,
    norm_gain,
    router,
    slot_expert,
    expert_ids,
    gate_up,
    down,
):
    n = lax.axis_size("node")
    rows, features = resid.shape
    capacity = prev_rows.shape[3]
    units = down.shape[1]
    strips = units // LANES
    depth = n // 4
    tokens = n * rows
    smem = pl.BlockSpec(memory_space=pltpu.SMEM)
    vmem = pl.BlockSpec(memory_space=pltpu.VMEM)
    anywhere = pl.BlockSpec(memory_space=pl.ANY)
    block = (rows, features)
    dma = pltpu.SemaphoreType.DMA
    attended_shape = query.shape[:2] + (LATENT,)
    attended, mixed = pl.pallas_call(
        functools.partial(fused_kernel, n),
        out_shape=(
            jax.ShapeDtypeStruct(attended_shape, BF16),
            jax.ShapeDtypeStruct(block, F32),
        ),
        in_specs=[smem, smem] + [vmem] * 6 + [anywhere] * 5,
        out_specs=(anywhere, vmem),
        scratch_shapes=[
            pltpu.VMEM((n, capacity, features), BF16),
            pltpu.VMEM((n * capacity, features), F32),
            pltpu.VMEM(query.shape, BF16),
            pltpu.VMEM(cache.shape, BF16),
            pltpu.VMEM(attended_shape, BF16),
            pltpu.VMEM((strips, features, 2, LANES), BF16),
            pltpu.VMEM((units, features), BF16),
            pltpu.VMEM((n, rows, features + LANES), BF16),
            pltpu.VMEM((features, units), BF16),
            pltpu.VMEM((features, units), BF16),
            pltpu.VMEM((tokens, features), BF16),
            pltpu.VMEM((strips // 2, tokens, 2 * LANES), BF16),
            pltpu.VMEM((n,) + block, F32),
            pltpu.VMEM((n,) + block, BF16),
            pltpu.VMEM((2 * depth,) + block, BF16),
            pltpu.VMEM((depth,) + block, BF16),
            pltpu.VMEM((depth,) + block, BF16),
            pltpu.VMEM((depth,) + block, BF16),
            pltpu.VMEM((depth,) + block, BF16),
            pltpu.VMEM(block, F32),
            dma((5,)),
            dma((strips,)),
            dma((n,)),
            dma((n,)),
            dma((n,)),
            dma((n,)),
            dma((n,)),
            dma((n,)),
        ],
        compiler_params=pltpu.CompilerParams(
            collective_id=0, has_side_effects=True, vmem_limit_bytes=58 * 2**20
        ),
        name="fused_step",
    )(
        lengths,
        slot_expert,
        resid,
        prev_slots.T,
        prev_gates.T,
        norm_gain,
        router.T,
        expert_ids.T,
        prev_rows,
        query,
        cache,
        gate_up,
        down,
    )
    return attended, mixed.astype(BF16)


def solution(mesh):
    fused = mesh.shape["local"] == 1 and mesh.shape["node"] % 4 == 0
    return jax.shard_map(
        fused_shards if fused else shards,
        mesh=mesh,
        in_specs=(
            P(("groups", "node", "local"), None),
            P(("groups", "node"), "local", None, None, None),
            P(("groups", "node", "local"), None),
            P(("groups", "node", "local"), None),
            P(("groups", "node", "local"), None, None),
            P(("groups", "node", "local"), None, None),
            P(("groups", "node", "local")),
            P(),
            P(),
            P(),
            P(("groups", "node", "local"), None),
            P("node", None, None, "local"),
            P("node", "local", None),
        ),
        out_specs=(
            P(("groups", "node", "local"), None, None),
            P(("groups", "node", "local"), None),
        ),
        check_vma=False,
    )
```
